32 devices in a mesh: fsdp: 8 (over z, x), tp: 4 (over y, core).
Axes of the slice: x: 2, y: 2, z: 4, core: 2. Of those that a mesh axis runs over, the one named last changes fastest.
Arguments:
- grad_out: bfloat16 [2048, 8192], P('fsdp', 'tp'), may hold values from -6 to 6
- down_q: bfloat16 [14336, 8192], P('fsdp', 'tp'), may hold values from -0.0625 to 0.0625
- scales: bfloat16 [112, 64], P('fsdp', 'tp'), may hold values from 0.25 to 4
- gate_act: bfloat16 [2048, 14336], P('fsdp', 'tp'), may hold values from -6 to 6
- up_act: bfloat16 [2048, 14336], P('fsdp', 'tp'), may hold values from -6 to 6
Outputs:
- grad_gate: bfloat16 [2048, 14336], P('fsdp', 'tp')
- grad_up: bfloat16 [2048, 14336], P('fsdp', 'tp')
The draws below stay inside these ranges and needn't reach their ends.
All inputs are finite; a program needn't handle non-finite values.
Results may differ from the reference program's by a relative error of at most 0.005.
Values may be sent and summed in bfloat16 or wider, within the bound.
A program may use at most 192 MiB of HBM per device.

```python
import math
import jax
import jax.numpy as jnp
from jax import lax

D = 8192
FF = 14336
BLOCK = 128
TOKENS = 2048


def block_levels(rng, dims, pieces, least, high):
    factor_of, own = 1.0, jax.random.fold_in(rng, 6)
    for axis_at, parts in pieces:
        draws = jnp.exp(jax.random.uniform(jax.random.fold_in(own, axis_at), (parts,), jnp.float32, least / len(pieces), high / len(pieces)))
        factor_of = factor_of * jnp.repeat(draws, dims[axis_at] // parts).reshape([-1 if axis == axis_at else 1 for axis in range(len(dims))])
    return factor_of


def centred(stream_key, dims, width, most, cuts=(), kind=jnp.bfloat16):
    loudness = block_levels(stream_key, dims, cuts, -0.22, 0.18) if cuts else 1.0
    drawn = jax.random.normal(stream_key, dims, jnp.float32) * width * loudness
    return jnp.minimum(jnp.maximum(drawn, -most), most).astype(kind)


def setup_inputs(seed: int = 0) -> dict:
    arg_keys = jax.random.split(jax.random.key(seed), 6)
    grad_out = centred(arg_keys[0], (TOKENS, D), 1.0, 6.0, ((0, 8), (1, 4)))
    down_q = centred(arg_keys[1], (FF, D), D ** -0.5, 0.0625, ((0, 8), (1, 4)))
    scales = jnp.clip(jnp.exp(math.log(4.0) - 2.7725887 * jax.random.uniform(arg_keys[2], (FF // BLOCK, D // BLOCK), jnp.float32) ** block_levels(arg_keys[2], (FF // BLOCK, D // BLOCK), ((0, 8), (1, 4)), -0.2, 0.2)), 0.25, 4.0).astype(jnp.bfloat16)
    gate_act = centred(arg_keys[3], (TOKENS, FF), 1.5, 6.0, ((0, 8), (1, 4)))
    up_act = centred(arg_keys[4], (TOKENS, FF), 1.0, 6.0, ((0, 8), (1, 4)))
    return dict(grad_out=grad_out, down_q=down_q, scales=scales, gate_act=gate_act, up_act=up_act)


def dequantize(values, scales):
    rows, cols = values.shape
    grid = values.astype(jnp.float32).reshape(rows // BLOCK, BLOCK, cols // BLOCK, BLOCK)
    grid = grid * scales.astype(jnp.float32)[:, None, :, None]
    return grid.reshape(rows, cols).astype(jnp.bfloat16)


def reference(grad_out, down_q, scales, gate_act, up_act):
    weight = dequantize(down_q, scales)
    grad_hidden = lax.dot_general(grad_out, weight, (((1,), (1,)), ((), ())), preferred_element_type=jnp.float32)
    gate_val = gate_act.astype(jnp.float32)
    sigmoid_gate = jax.nn.sigmoid(gate_val)
    grad_up = (grad_hidden * gate_val * sigmoid_gate).astype(jnp.bfloat16)
    slope = sigmoid_gate * (1.0 + gate_val * (1.0 - sigmoid_gate))
    grad_gate = (grad_hidden * up_act.astype(jnp.float32) * slope).astype(jnp.bfloat16)
    return grad_gate, grad_up
```

```python
import jax
import jax.numpy as jnp
from jax import lax
from jax.sharding import PartitionSpec as P

BLOCK = 128


def dequantize(values, scales):
    rows, cols = values.shape
    grid = values.astype(jnp.float32).reshape(rows // BLOCK, BLOCK, cols // BLOCK, BLOCK)
    grid = grid * scales.astype(jnp.float32)[:, None, :, None]
    return grid.reshape(rows, cols).astype(jnp.bfloat16)


def on_device(F, T, grad_out, down_q, scales, gate_act, up_act):
    R = F // T
    f = lax.axis_index("fsdp")
    rows = grad_out.shape[0]
    hidden = down_q.shape[0]
    weight = dequantize(down_q, scales)
    tokens = lax.all_gather(grad_out, "fsdp", axis=0, tiled=True)
    partial_value = lax.dot_general(
        tokens, weight, (((1,), (1,)), ((), ())), preferred_element_type=jnp.float32
    ).astype(jnp.bfloat16)
    mine = lax.psum_scatter(partial_value, "tp", scatter_dimension=0, tiled=True)
    mine = mine.reshape(R, rows, hidden)
    own_f = lax.axis_index("fsdp")
    grad_hidden = jnp.zeros((rows, R, hidden), jnp.bfloat16)
    for s in range(R):
        pairs = []
        for a in range(F):
            for b in range(T):
                j = (a + s) % R
                pairs.append((a * T + b, (R * b + j) * T + a // R))
        piece = lax.dynamic_index_in_dim(mine, (own_f + s) % R, 0, keepdims=False)
        got = lax.ppermute(piece, ("fsdp", "tp"), pairs)
        i = (own_f - s) % R
        grad_hidden = lax.dynamic_update_slice(grad_hidden, got[:, None, :], (0, i, 0))
    grad_hidden = grad_hidden.reshape(rows, R * hidden).astype(jnp.float32)
    gate_val = gate_act.astype(jnp.float32)
    sigmoid_gate = jax.nn.sigmoid(gate_val)
    grad_up = (grad_hidden * gate_val * sigmoid_gate).astype(jnp.bfloat16)
    slope = sigmoid_gate * (1.0 + gate_val * (1.0 - sigmoid_gate))
    grad_gate = (grad_hidden * up_act.astype(jnp.float32) * slope).astype(jnp.bfloat16)
    return (grad_gate, grad_up)


def solution(mesh):
    F, T = mesh.shape["fsdp"], mesh.shape["tp"]

    def body(*args):
        return on_device(F, T, *args)

    spec = P("fsdp", "tp")
    return jax.shard_map(
        body, mesh=mesh, in_specs=(spec,) * 5, out_specs=(spec, spec), check_vma=False
    )
```

```python
import functools

import jax
import jax.numpy as jnp
from jax import lax
from jax.experimental import pallas as pl
from jax.experimental.pallas import tpu as pltpu
from jax.sharding import PartitionSpec as P

BLOCK = 128
X = 2
LAG_X = 2
LAG_SUM = 2
MESH = pl.DeviceIdType.MESH


def kernel(F, T, a_ref, q_ref, s_ref, out_ref, ga, w, part, tile, acc, rbuf, fin,
           lsem, gr, up, dn, xs, ts, tr, fs, fr):
    R, Z = F // T, F // X
    tb = a_ref.shape[0]
    hb = q_ref.shape[0]
    pb = tb // T
    wide = 256 if hb % 256 == 0 else 128
    f, t = lax.axis_index("fsdp"), lax.axis_index("tp")
    z, x = lax.div(f, X), lax.rem(f, X)
    xpeer = f + 1 - 2 * x
    owner_t, owner_i = lax.div(f, R), lax.rem(f, R)
    to_self = owner_t == t

    copy_a = pltpu.make_async_copy(a_ref, ga.at[f], lsem.at[0])
    copy_q = pltpu.make_async_copy(q_ref, w, lsem.at[1])
    copy_a.start()
    copy_q.start()

    barrier = pltpu.get_barrier_semaphore()

    def greet(df, dt):
        pl.semaphore_signal(barrier, inc=1, device_id=(df, dt), device_id_type=MESH)

    @pl.when(z > 0)
    def _():
        greet(f - X, t)

    @pl.when(z < Z - 1)
    def _():
        greet(f + X, t)

    greet(xpeer, t)
    for o in range(1, T):
        greet(f, lax.rem(t + o, T))

    for i in range(R):
        @pl.loop(0, T)
        def _(t2):
            @pl.when(jnp.logical_not((t * R + i == f) & (t2 == t)))
            def _():
                greet(t * R + i, t2)

    waits = 1 + (T - 1) + F
    waits = waits + (z > 0).astype(jnp.int32) + (z < Z - 1).astype(jnp.int32)
    pl.semaphore_wait(barrier, waits - to_self.astype(jnp.int32))

    def gather_copy(zz, sem, df):
        slot = zz * X + x
        return pltpu.make_async_remote_copy(
            src_ref=ga.at[slot], dst_ref=ga.at[slot], send_sem=sem.at[zz],
            recv_sem=gr.at[slot], device_id=(df, t), device_id_type=MESH)

    def gather_recv(slot):
        pltpu.make_async_remote_copy(
            src_ref=ga.at[slot], dst_ref=ga.at[slot], send_sem=xs.at[0],
            recv_sem=gr.at[slot], device_id=(xpeer, t), device_id_type=MESH).wait_recv()

    def forward(zz, act):
        @pl.when((zz <= z) & (z < Z - 1))
        def _():
            act(gather_copy(zz, up, f + X))

        @pl.when((zz >= z) & (z > 0))
        def _():
            act(gather_copy(zz, dn, f - X))

        act(gather_copy(zz, xs, xpeer))

    def tp_copy(slot, t2):
        return pltpu.make_async_remote_copy(
            src_ref=part.at[slot, pl.ds(pl.multiple_of(t2 * pb, pb), pb), :],
            dst_ref=rbuf.at[slot, t], send_sem=ts.at[slot, t2],
            recv_sem=tr.at[slot, t], device_id=(f, t2), device_id_type=MESH)

    def tp_recv(slot, t2):
        pltpu.make_async_remote_copy(
            src_ref=rbuf.at[slot, t2], dst_ref=rbuf.at[slot, t2], send_sem=ts.at[slot, t2],
            recv_sem=tr.at[slot, t2], device_id=(f, t2), device_id_type=MESH).wait_recv()

    def out_at(i, t2):
        return out_ref.at[pl.ds(pl.multiple_of(t2 * pb, pb), pb),
                          pl.ds(pl.multiple_of(i * hb, 128), hb)]

    def fin_remote(slot):
        return pltpu.make_async_remote_copy(
            src_ref=fin.at[slot], dst_ref=out_at(owner_i, t), send_sem=fs.at[slot],
            recv_sem=fr.at[owner_i, t], device_id=(slot, owner_t), device_id_type=MESH)

    def fin_local():
        return pltpu.make_async_copy(fin.at[f], out_at(owner_i, t), lsem.at[2])

    def multiply(slot):
        @pl.loop(0, hb // wide)
        def _(n):
            at = pl.ds(pl.multiple_of(n * wide, wide), wide)
            prod = lax.dot_general(ga[slot], w[at, :], (((1,), (1,)), ((), ())),
                                   preferred_element_type=jnp.float32)
            tile[:, at] = prod
            part[slot, :, at] = prod.astype(jnp.bfloat16)

        acc[slot] = tile[pl.ds(pl.multiple_of(t * pb, pb), pb), :]
        for o in range(1, T):
            tp_copy(slot, lax.rem(t + o, T)).start()

    def add_up(slot):
        for o in range(1, T):
            tp_recv(slot, lax.rem(t + o, T))
        total = acc[slot]
        for o in range(1, T):
            total = total + rbuf[slot, lax.rem(t + o, T)].astype(jnp.float32)
        fin[slot] = total.astype(jnp.bfloat16)
        own = to_self & (slot == f)

        @pl.when(own)
        def _():
            fin_local().start()

        @pl.when(jnp.logical_not(own))
        def _():
            fin_remote(slot).start()

    copy_a.wait()
    forward(z, lambda c: c.start())
    copy_q.wait()

    @pl.loop(0, hb // BLOCK)
    def _(b):
        at = pl.ds(pl.multiple_of(b * BLOCK, BLOCK), BLOCK)
        w[at, :] = (w[at, :].astype(jnp.float32) * s_ref[pl.ds(b, 1), :]).astype(jnp.bfloat16)

    steps = 2 * Z - 1

    def when_valid(k, body):
        d = lax.div(k + 1, 2)
        zz = z + d * (1 - 2 * lax.rem(k, 2))

        @pl.when((k >= 0) & (k < steps) & (zz >= 0) & (zz < Z))
        def _():
            body(zz)

    def own_column(zz):
        slot = zz * X + x

        @pl.when(zz != z)
        def _():
            gather_recv(slot)
            forward(zz, lambda c: c.start())

        multiply(slot)

    def other_column(zz):
        slot = zz * X + 1 - x
        gather_recv(slot)
        multiply(slot)

    @pl.loop(0, steps + LAG_X + LAG_SUM)
    def _(i):
        when_valid(i, own_column)
        when_valid(i - LAG_SUM, lambda zz: add_up(zz * X + x))
        when_valid(i - LAG_X, other_column)
        when_valid(i - LAG_X - LAG_SUM, lambda zz: add_up(zz * X + 1 - x))

    @pl.loop(0, Z)
    def _(zz):
        forward(zz, lambda c: c.wait_send())

    @pl.loop(0, F)
    def _(slot):
        for o in range(1, T):
            tp_copy(slot, lax.rem(t + o, T)).wait_send()
        own = to_self & (slot == f)

        @pl.when(own)
        def _():
            fin_local().wait()

        @pl.when(jnp.logical_not(own))
        def _():
            fin_remote(slot).wait_send()

    for i in range(R):
        @pl.loop(0, T)
        def _(t2):
            @pl.when(jnp.logical_not((t * R + i == f) & (t2 == t)))
            def _():
                pltpu.make_async_remote_copy(
                    src_ref=fin.at[0], dst_ref=out_at(i, t2), send_sem=fs.at[0],
                    recv_sem=fr.at[i, t2], device_id=(t * R + i, t2),
                    device_id_type=MESH).wait_recv()


def hidden_gradient(F, T, grad_out, down_q, scales):
    R, Z = F // T, F // X
    tb, kd = grad_out.shape
    hb = down_q.shape[0]
    pb = tb // T
    wide_scales = jnp.repeat(scales.astype(jnp.float32), BLOCK, axis=1)
    any_spec = pl.BlockSpec(memory_space=pl.ANY)
    return pl.pallas_call(
        functools.partial(kernel, F, T),
        out_shape=jax.ShapeDtypeStruct((tb, R * hb), jnp.bfloat16),
        in_specs=[any_spec, any_spec, pl.BlockSpec(memory_space=pltpu.VMEM)],
        out_specs=any_spec,
        scratch_shapes=[
            pltpu.VMEM((F, tb, kd), jnp.bfloat16),
            pltpu.VMEM((hb, kd), jnp.bfloat16),
            pltpu.VMEM((F, tb, hb), jnp.bfloat16),
            pltpu.VMEM((tb, hb), jnp.float32),
            pltpu.VMEM((F, pb, hb), jnp.float32),
            pltpu.VMEM((F, T, pb, hb), jnp.bfloat16),
            pltpu.VMEM((F, pb, hb), jnp.bfloat16),
            pltpu.SemaphoreType.DMA((3,)),
            pltpu.SemaphoreType.DMA((F,)),
            pltpu.SemaphoreType.DMA((Z,)),
            pltpu.SemaphoreType.DMA((Z,)),
            pltpu.SemaphoreType.DMA((Z,)),
            pltpu.SemaphoreType.DMA((F, T)),
            pltpu.SemaphoreType.DMA((F, T)),
            pltpu.SemaphoreType.DMA((F,)),
            pltpu.SemaphoreType.DMA((R, T)),
        ],
        compiler_params=pltpu.CompilerParams(
            collective_id=0, has_side_effects=True, vmem_limit_bytes=56 * 2**20),
        cost_estimate=pl.CostEstimate(
            flops=2 * F * tb * kd * hb, bytes_accessed=2 * hb * (kd + R * tb),
            transcendentals=0),
    )(grad_out, down_q, wide_scales)


def on_device(F, T, grad_out, down_q, scales, gate_act, up_act):
    grad_hidden = hidden_gradient(F, T, grad_out, down_q, scales).astype(jnp.float32)
    gate_val = gate_act.astype(jnp.float32)
    sigmoid_gate = jax.nn.sigmoid(gate_val)
    grad_up = (grad_hidden * gate_val * sigmoid_gate).astype(jnp.bfloat16)
    slope = sigmoid_gate * (1.0 + gate_val * (1.0 - sigmoid_gate))
    grad_gate = (grad_hidden * up_act.astype(jnp.float32) * slope).astype(jnp.bfloat16)
    return (grad_gate, grad_up)


def solution(mesh):
    F, T = mesh.shape["fsdp"], mesh.shape["tp"]
    spec = P("fsdp", "tp")
    return jax.shard_map(
        functools.partial(on_device, F, T),
        mesh=mesh, in_specs=(spec,) * 5, out_specs=(spec, spec), check_vma=False)
```

```python
import functools
import math

import jax
import jax.numpy as jnp
from jax import lax
from jax.experimental import pallas as pl
from jax.experimental.pallas import tpu as pltpu
from jax.sharding import PartitionSpec as P

BLOCK = 128
X = 2
CORES = 2
CHUNKS = 2
LAG_X = 3
LAG_SUM = 2
MESH = pl.DeviceIdType.MESH


def kernel(F, T, aligned, a_ref, q_ref, s_ref, out_ref, ga, q, w, part, tile, acc, rbuf, fin,
           lsem, wsem, gr, up, dn, xs, sr, ss, ts, tr, fs, fr):
    R, Z, U = F // T, F // X, T // CORES
    tb, kd = a_ref.shape
    hb = q_ref.shape[0]
    hh = hb // CORES
    pb, cb = tb // U, tb // CHUNKS
    f, t = lax.axis_index("fsdp"), lax.axis_index("tp")
    z, x = lax.div(f, X), lax.rem(f, X)
    u, c = lax.div(t, CORES), lax.rem(t, CORES)
    xpeer, sibling = f + 1 - 2 * x, t + 1 - 2 * c
    owner_t, owner_i = lax.div(f, R), lax.rem(f, R)
    to_self = owner_t == t
    mine = pl.ds(pl.multiple_of(c * kd, 128), kd)
    theirs = pl.ds(pl.multiple_of((1 - c) * kd, 128), kd)

    copy_a = pltpu.make_async_copy(a_ref, ga.at[f, :, mine], lsem.at[0])
    copy_q = pltpu.make_async_copy(q_ref, q, lsem.at[1])
    copy_a.start()
    copy_q.start()

    barrier = pltpu.get_barrier_semaphore()

    def greet(df, dt):
        pl.semaphore_signal(barrier, inc=1, device_id=(df, dt), device_id_type=MESH)

    @pl.when(z > 0)
    def _():
        greet(f - X, t)

    @pl.when(z < Z - 1)
    def _():
        greet(f + X, t)

    greet(xpeer, t)
    greet(f, sibling)

    def peer(o):
        return lax.rem(u + o, U)

    for o in range(1, U):
        greet(f, peer(o) * CORES + c)

    for i in range(R):
        @pl.loop(0, T)
        def _(t2):
            @pl.when(jnp.logical_not((t * R + i == f) & (t2 == t)))
            def _():
                greet(t * R + i, t2)

    waits = 2 + (U - 1) + F
    waits = waits + (z > 0).astype(jnp.int32) + (z < Z - 1).astype(jnp.int32)
    pl.semaphore_wait(barrier, waits - to_self.astype(jnp.int32))

    def shard(slot, j, lanes):
        return ga.at[slot, pl.ds(pl.multiple_of(j * cb, cb), cb), lanes]

    def gather_copy(zz, j, sem, df):
        slot = zz * X + x
        ref = shard(slot, j, mine)
        return pltpu.make_async_remote_copy(
            src_ref=ref, dst_ref=ref, send_sem=sem.at[zz, j],
            recv_sem=gr.at[slot, j], device_id=(df, t), device_id_type=MESH)

    def gather_recv(slot, j):
        ref = shard(slot, j, mine)
        pltpu.make_async_remote_copy(
            src_ref=ref, dst_ref=ref, send_sem=xs.at[0, 0],
            recv_sem=gr.at[slot, j], device_id=(xpeer, t), device_id_type=MESH).wait_recv()

    def share_copy(slot, j):
        ref = shard(slot, j, mine)
        return pltpu.make_async_remote_copy(
            src_ref=ref, dst_ref=ref, send_sem=ss.at[slot, j],
            recv_sem=sr.at[slot, j], device_id=(f, sibling), device_id_type=MESH)

    def share_recv(slot, j):
        ref = shard(slot, j, theirs)
        pltpu.make_async_remote_copy(
            src_ref=ref, dst_ref=ref, send_sem=ss.at[slot, j],
            recv_sem=sr.at[slot, j], device_id=(f, sibling), device_id_type=MESH).wait_recv()

    def forward(zz, j, act):
        @pl.when((zz <= z) & (z < Z - 1))
        def _():
            act(gather_copy(zz, j, up, f + X))

        @pl.when((zz >= z) & (z > 0))
        def _():
            act(gather_copy(zz, j, dn, f - X))

        act(gather_copy(zz, j, xs, xpeer))

    def sum_copy(slot, u2):
        return pltpu.make_async_remote_copy(
            src_ref=part.at[slot, pl.ds(pl.multiple_of(u2 * pb, pb), pb), :],
            dst_ref=rbuf.at[slot, u], send_sem=ts.at[slot, u2],
            recv_sem=tr.at[slot, u], device_id=(f, u2 * CORES + c), device_id_type=MESH)

    def sum_recv(slot, u2):
        pltpu.make_async_remote_copy(
            src_ref=rbuf.at[slot, u2], dst_ref=rbuf.at[slot, u2], send_sem=ts.at[slot, u2],
            recv_sem=tr.at[slot, u2], device_id=(f, u2 * CORES + c),
            device_id_type=MESH).wait_recv()

    def out_at(i, t2):
        rows = pl.ds(pl.multiple_of(lax.div(t2, CORES) * pb, pb), pb)
        half = lax.rem(t2, CORES)
        if aligned:
            return out_ref.at[rows, pl.ds(pl.multiple_of(i * hb + half * hh, 128), hh)]
        return out_ref.at[i * CORES + half, rows, :]

    def fin_remote(slot):
        return pltpu.make_async_remote_copy(
            src_ref=fin.at[slot], dst_ref=out_at(owner_i, t), send_sem=fs.at[slot],
            recv_sem=fr.at[owner_i, t], device_id=(slot, owner_t), device_id_type=MESH)

    def fin_local():
        return pltpu.make_async_copy(fin.at[f], out_at(owner_i, t), lsem.at[2])

    def multiply(slot):
        for j in range(CHUNKS):
            share_recv(slot, j)
        for lo in range(0, hh, 256):
            n = min(256, hh - lo)
            prod = lax.dot_general(ga[slot], w[lo:lo + n, :], (((1,), (1,)), ((), ())),
                                   preferred_element_type=jnp.float32)
            tile[:, lo:lo + n] = prod
            part[slot, :, lo:lo + n] = prod.astype(jnp.bfloat16)
        for o in range(1, U):
            sum_copy(slot, peer(o)).start()
        acc[slot] = tile[pl.ds(pl.multiple_of(u * pb, pb), pb), :]

    def add_up(slot):
        for o in range(1, U):
            sum_recv(slot, peer(o))
        total = acc[slot]
        for o in range(1, U):
            total = total + rbuf[slot, peer(o)].astype(jnp.float32)
        fin[slot] = total.astype(jnp.bfloat16)
        own = to_self & (slot == f)

        @pl.when(own)
        def _():
            fin_local().start()

        @pl.when(jnp.logical_not(own))
        def _():
            fin_remote(slot).start()

    def start(copy):
        copy.start()

    copy_a.wait()
    for j in range(CHUNKS):
        forward(z, j, start)
    for j in range(CHUNKS):
        share_copy(f, j).start()
    copy_q.wait()

    rows = math.gcd(hh, BLOCK)
    other = (1 - c) * hh
    give = pltpu.make_async_remote_copy(
        src_ref=q.at[pl.ds(pl.multiple_of(other, rows), hh), :], dst_ref=w.at[:, mine],
        send_sem=wsem.at[0], recv_sem=wsem.at[1], device_id=(f, sibling), device_id_type=MESH)

    def scaled(r):
        at = pl.ds(pl.multiple_of(r, rows), rows)
        return (q[at, :].astype(jnp.float32)
                * s_ref[pl.ds(lax.div(r, BLOCK), 1), :]).astype(jnp.bfloat16)

    @pl.loop(0, hh // rows)
    def _(b):
        r = other + b * rows
        q[pl.ds(pl.multiple_of(r, rows), rows), :] = scaled(r)

    give.start()

    @pl.loop(0, hh // rows)
    def _(b):
        w[pl.ds(pl.multiple_of(b * rows, rows), rows), mine] = scaled(c * hh + b * rows)

    pltpu.make_async_remote_copy(
        src_ref=q.at[pl.ds(pl.multiple_of(other, rows), hh), :], dst_ref=w.at[:, theirs],
        send_sem=wsem.at[0], recv_sem=wsem.at[1], device_id=(f, sibling),
        device_id_type=MESH).wait_recv()

    steps = 2 * Z - 1

    def when_valid(k, body):
        d = lax.div(k + 1, 2)
        zz = z + d * (1 - 2 * lax.rem(k, 2))

        @pl.when((k >= 0) & (k < steps) & (zz >= 0) & (zz < Z))
        def _():
            body(zz)

    def own_column(zz):
        slot = zz * X + x

        @pl.when(zz != z)
        def _():
            for j in range(CHUNKS):
                gather_recv(slot, j)
                forward(zz, j, start)
                share_copy(slot, j).start()

        multiply(slot)

    def other_column(zz):
        slot = zz * X + 1 - x
        for j in range(CHUNKS):
            gather_recv(slot, j)
            share_copy(slot, j).start()
        multiply(slot)

    @pl.loop(0, steps + LAG_X + LAG_SUM)
    def _(i):
        when_valid(i, own_column)
        when_valid(i - LAG_X, other_column)
        when_valid(i - LAG_SUM, lambda zz: add_up(zz * X + x))
        when_valid(i - LAG_X - LAG_SUM, lambda zz: add_up(zz * X + 1 - x))

    give.wait_send()

    @pl.loop(0, Z)
    def _(zz):
        for j in range(CHUNKS):
            forward(zz, j, lambda copy: copy.wait_send())

    @pl.loop(0, F)
    def _(slot):
        for j in range(CHUNKS):
            share_copy(slot, j).wait_send()
        for o in range(1, U):
            sum_copy(slot, peer(o)).wait_send()
        own = to_self & (slot == f)

        @pl.when(own)
        def _():
            fin_local().wait()

        @pl.when(jnp.logical_not(own))
        def _():
            fin_remote(slot).wait_send()

    for i in range(R):
        @pl.loop(0, T)
        def _(t2):
            @pl.when(jnp.logical_not((t * R + i == f) & (t2 == t)))
            def _():
                pltpu.make_async_remote_copy(
                    src_ref=fin.at[0], dst_ref=out_at(i, t2), send_sem=fs.at[0],
                    recv_sem=fr.at[i, t2], device_id=(t * R + i, t2),
                    device_id_type=MESH).wait_recv()


def hidden_gradient(F, T, grad_out, down_q, scales):
    R, Z, U = F // T, F // X, T // CORES
    tb, kd = grad_out.shape
    hb = down_q.shape[0]
    hh, pb = hb // CORES, tb // U
    aligned = hh % 128 == 0
    out_shape = (tb, R * hb) if aligned else (R * CORES, tb, hh)
    wide_scales = jnp.repeat(scales.astype(jnp.float32), BLOCK, axis=1)
    any_spec = pl.BlockSpec(memory_space=pl.ANY)
    dma = pltpu.SemaphoreType.DMA
    out = pl.pallas_call(
        functools.partial(kernel, F, T, aligned),
        out_shape=jax.ShapeDtypeStruct(out_shape, jnp.bfloat16),
        in_specs=[any_spec, any_spec, pl.BlockSpec(memory_space=pltpu.VMEM)],
        out_specs=any_spec,
        scratch_shapes=[
            pltpu.VMEM((F, tb, CORES * kd), jnp.bfloat16),
            pltpu.VMEM((hb, kd), jnp.bfloat16),
            pltpu.VMEM((hh, CORES * kd), jnp.bfloat16),
            pltpu.VMEM((F, tb, hh), jnp.bfloat16),
            pltpu.VMEM((tb, hh), jnp.float32),
            pltpu.VMEM((F, pb, hh), jnp.float32),
            pltpu.VMEM((F, U, pb, hh), jnp.bfloat16),
            pltpu.VMEM((F, pb, hh), jnp.bfloat16),
            dma((3,)),
            dma((2,)),
            dma((F, CHUNKS)),
            dma((Z, CHUNKS)),
            dma((Z, CHUNKS)),
            dma((Z, CHUNKS)),
            dma((F, CHUNKS)),
            dma((F, CHUNKS)),
            dma((F, U)),
            dma((F, U)),
            dma((F,)),
            dma((R, T)),
        ],
        compiler_params=pltpu.CompilerParams(
            collective_id=0, has_side_effects=True, vmem_limit_bytes=58 * 2**20),
        cost_estimate=pl.CostEstimate(
            flops=2 * F * tb * kd * hb, bytes_accessed=2 * hb * (kd + R * tb),
            transcendentals=0),
    )(grad_out, down_q, wide_scales)
    if aligned:
        return out
    return out.transpose(1, 0, 2).reshape(tb, R * hb)


def on_device(F, T, grad_out, down_q, scales, gate_act, up_act):
    grad_hidden = hidden_gradient(F, T, grad_out, down_q, scales).astype(jnp.float32)
    gate_val = gate_act.astype(jnp.float32)
    sigmoid_gate = jax.nn.sigmoid(gate_val)
    grad_up = (grad_hidden * gate_val * sigmoid_gate).astype(jnp.bfloat16)
    slope = sigmoid_gate * (1.0 + gate_val * (1.0 - sigmoid_gate))
    grad_gate = (grad_hidden * up_act.astype(jnp.float32) * slope).astype(jnp.bfloat16)
    return (grad_gate, grad_up)


def solution(mesh):
    F, T = mesh.shape["fsdp"], mesh.shape["tp"]
    spec = P("fsdp", "tp")
    return jax.shard_map(
        functools.partial(on_device, F, T),
        mesh=mesh, in_specs=(spec,) * 5, out_specs=(spec, spec), check_vma=False)
```

```python
import functools
import math

import jax
import jax.numpy as jnp
from jax import lax
from jax.experimental import pallas as pl
from jax.experimental.pallas import tpu as pltpu
from jax.sharding import PartitionSpec as P

BLOCK = 128
X = 2
CORES = 2
CHUNKS = 2
LAG_X = 3
LAG_SUM = 2
MESH = pl.DeviceIdType.MESH


def kernel(F, T, aligned, a_ref, q_ref, s_ref, out_ref, ga, q, w, part, tile, acc, rbuf, fin,
           lsem, wsem, gr, up, dn, xs, sr, ss, ts, tr, fs, fr):
    R, Z, U = F // T, F // X, T // CORES
    tb, kd = a_ref.shape
    hb = q_ref.shape[0]
    hh = hb // CORES
    pb, cb = tb // U, tb // CHUNKS
    f, t = lax.axis_index("fsdp"), lax.axis_index("tp")
    z, x = lax.div(f, X), lax.rem(f, X)
    u, c = lax.div(t, CORES), lax.rem(t, CORES)
    xpeer, sibling = f + 1 - 2 * x, t + 1 - 2 * c
    owner_t, owner_i = lax.div(f, R), lax.rem(f, R)
    to_self = owner_t == t
    mine = pl.ds(pl.multiple_of(c * kd, 128), kd)
    theirs = pl.ds(pl.multiple_of((1 - c) * kd, 128), kd)

    copy_a = pltpu.make_async_copy(a_ref, ga.at[f, :, mine], lsem.at[0])
    copy_q = pltpu.make_async_copy(q_ref, q, lsem.at[1])
    copy_a.start()
    copy_q.start()

    barrier = pltpu.get_barrier_semaphore()

    def greet(df, dt):
        pl.semaphore_signal(barrier, inc=1, device_id=(df, dt), device_id_type=MESH)

    @pl.when(z > 0)
    def _():
        greet(f - X, t)

    @pl.when(z < Z - 1)
    def _():
        greet(f + X, t)

    greet(xpeer, t)
    greet(f, sibling)

    def peer(o):
        return lax.rem(u + o, U)

    for o in range(1, U):
        greet(f, peer(o) * CORES + c)

    for i in range(R):
        @pl.loop(0, T)
        def _(t2):
            @pl.when(jnp.logical_not((t * R + i == f) & (t2 == t)))
            def _():
                greet(t * R + i, t2)

    waits = 2 + (U - 1) + F
    waits = waits + (z > 0).astype(jnp.int32) + (z < Z - 1).astype(jnp.int32)
    pl.semaphore_wait(barrier, waits - to_self.astype(jnp.int32))

    def shard(slot, j, lanes):
        return ga.at[slot, pl.ds(pl.multiple_of(j * cb, cb), cb), lanes]

    def gather_copy(zz, j, sem, df):
        slot = zz * X + x
        ref = shard(slot, j, mine)
        return pltpu.make_async_remote_copy(
            src_ref=ref, dst_ref=ref, send_sem=sem.at[zz, j],
            recv_sem=gr.at[slot, j], device_id=(df, t), device_id_type=MESH)

    def gather_recv(slot, j):
        ref = shard(slot, j, mine)
        pltpu.make_async_remote_copy(
            src_ref=ref, dst_ref=ref, send_sem=xs.at[0, 0],
            recv_sem=gr.at[slot, j], device_id=(xpeer, t), device_id_type=MESH).wait_recv()

    def share_copy(slot, j):
        ref = shard(slot, j, mine)
        return pltpu.make_async_remote_copy(
            src_ref=ref, dst_ref=ref, send_sem=ss.at[slot, j],
            recv_sem=sr.at[slot, j], device_id=(f, sibling), device_id_type=MESH)

    def share_recv(slot, j):
        ref = shard(slot, j, theirs)
        pltpu.make_async_remote_copy(
            src_ref=ref, dst_ref=ref, send_sem=ss.at[slot, j],
            recv_sem=sr.at[slot, j], device_id=(f, sibling), device_id_type=MESH).wait_recv()

    def forward(zz, j, act):
        @pl.when((zz <= z) & (z < Z - 1))
        def _():
            act(gather_copy(zz, j, up, f + X))

        @pl.when((zz >= z) & (z > 0))
        def _():
            act(gather_copy(zz, j, dn, f - X))

        act(gather_copy(zz, j, xs, xpeer))

    def sum_copy(slot, u2):
        return pltpu.make_async_remote_copy(
            src_ref=part.at[slot, pl.ds(pl.multiple_of(u2 * pb, pb), pb), :],
            dst_ref=rbuf.at[slot, u], send_sem=ts.at[slot, u2],
            recv_sem=tr.at[slot, u], device_id=(f, u2 * CORES + c), device_id_type=MESH)

    def sum_recv(slot, u2):
        pltpu.make_async_remote_copy(
            src_ref=rbuf.at[slot, u2], dst_ref=rbuf.at[slot, u2], send_sem=ts.at[slot, u2],
            recv_sem=tr.at[slot, u2], device_id=(f, u2 * CORES + c),
            device_id_type=MESH).wait_recv()

    def out_at(i, t2):
        rows = pl.ds(pl.multiple_of(lax.div(t2, CORES) * pb, pb), pb)
        half = lax.rem(t2, CORES)
        if aligned:
            return out_ref.at[rows, pl.ds(pl.multiple_of(i * hb + half * hh, 128), hh)]
        return out_ref.at[i * CORES + half, rows, :]

    def fin_remote(slot):
        return pltpu.make_async_remote_copy(
            src_ref=fin.at[slot], dst_ref=out_at(owner_i, t), send_sem=fs.at[slot],
            recv_sem=fr.at[owner_i, t], device_id=(slot, owner_t), device_id_type=MESH)

    def fin_local():
        return pltpu.make_async_copy(fin.at[f], out_at(owner_i, t), lsem.at[2])

    def multiply(slot):
        for j in range(CHUNKS):
            share_recv(slot, j)
        for lo in range(0, hh, 256):
            n = min(256, hh - lo)
            prod = lax.dot_general(ga[slot], w[lo:lo + n, :], (((1,), (1,)), ((), ())),
                                   preferred_element_type=jnp.float32)
            tile[:, lo:lo + n] = prod
            part[slot, :, lo:lo + n] = prod.astype(jnp.bfloat16)
        for o in range(1, U):
            sum_copy(slot, peer(o)).start()
        acc[slot] = tile[pl.ds(pl.multiple_of(u * pb, pb), pb), :]

    def add_up(slot):
        for o in range(1, U):
            sum_recv(slot, peer(o))
        total = acc[slot]
        for o in range(1, U):
            total = total + rbuf[slot, peer(o)].astype(jnp.float32)
        fin[slot] = total.astype(jnp.bfloat16)

    def send_sum(slot):
        own = to_self & (slot == f)

        @pl.when(own)
        def _():
            fin_local().start()

        @pl.when(jnp.logical_not(own))
        def _():
            fin_remote(slot).start()

    def start(copy):
        copy.start()

    copy_a.wait()
    for j in range(CHUNKS):
        forward(z, j, start)
    for j in range(CHUNKS):
        share_copy(f, j).start()
    copy_q.wait()

    rows = math.gcd(hh, BLOCK)
    other = (1 - c) * hh
    give = pltpu.make_async_remote_copy(
        src_ref=q.at[pl.ds(pl.multiple_of(other, rows), hh), :], dst_ref=w.at[:, mine],
        send_sem=wsem.at[0], recv_sem=wsem.at[1], device_id=(f, sibling), device_id_type=MESH)

    def scaled(r):
        at = pl.ds(pl.multiple_of(r, rows), rows)
        return (q[at, :].astype(jnp.float32)
                * s_ref[pl.ds(lax.div(r, BLOCK), 1), :]).astype(jnp.bfloat16)

    @pl.loop(0, hh // rows)
    def _(b):
        r = other + b * rows
        q[pl.ds(pl.multiple_of(r, rows), rows), :] = scaled(r)

    give.start()

    @pl.loop(0, hh // rows)
    def _(b):
        w[pl.ds(pl.multiple_of(b * rows, rows), rows), mine] = scaled(c * hh + b * rows)

    pltpu.make_async_remote_copy(
        src_ref=q.at[pl.ds(pl.multiple_of(other, rows), hh), :], dst_ref=w.at[:, theirs],
        send_sem=wsem.at[0], recv_sem=wsem.at[1], device_id=(f, sibling),
        device_id_type=MESH).wait_recv()

    steps = 2 * Z - 1

    below, above = z, Z - 1 - z
    last = jnp.where(above >= below, 2 * above, 2 * below - 1)
    near = (below == above) | (below == above + 1)
    before_last = last - jnp.where(near, 1, 2)

    def when_valid(k, body):
        d = lax.div(k + 1, 2)
        zz = z + d * (1 - 2 * lax.rem(k, 2))

        @pl.when((k >= 0) & (k < steps) & (zz >= 0) & (zz < Z))
        def _():
            body(zz, k)

    def send_held(column):
        @pl.loop(0, steps)
        def _(k):
            @pl.when(k + LAG_SUM < last)
            def _():
                when_valid(k, lambda zz, _: send_sum(zz * X + column))

    def own_column(zz, k):
        slot = zz * X + x

        @pl.when(zz != z)
        def _():
            for j in range(CHUNKS):
                gather_recv(slot, j)
                forward(zz, j, start)
                share_copy(slot, j).start()

        multiply(slot)

    def other_column(zz, k):
        slot = zz * X + 1 - x
        for j in range(CHUNKS):
            gather_recv(slot, j)
            share_copy(slot, j).start()

        @pl.when(k == before_last)
        def _():
            send_held(x)

        @pl.when(k == last)
        def _():
            send_held(1 - x)

        multiply(slot)

    def sum_column(column):
        def body(zz, k):
            add_up(zz * X + column)

            @pl.when(k + LAG_SUM >= last)
            def _():
                send_sum(zz * X + column)

        return body

    @pl.loop(0, steps + LAG_X + LAG_SUM)
    def _(i):
        when_valid(i, own_column)
        when_valid(i - LAG_X, other_column)
        when_valid(i - LAG_SUM, sum_column(x))
        when_valid(i - LAG_X - LAG_SUM, sum_column(1 - x))

    give.wait_send()

    @pl.loop(0, Z)
    def _(zz):
        for j in range(CHUNKS):
            forward(zz, j, lambda copy: copy.wait_send())

    @pl.loop(0, F)
    def _(slot):
        for j in range(CHUNKS):
            share_copy(slot, j).wait_send()
        for o in range(1, U):
            sum_copy(slot, peer(o)).wait_send()
        own = to_self & (slot == f)

        @pl.when(own)
        def _():
            fin_local().wait()

        @pl.when(jnp.logical_not(own))
        def _():
            fin_remote(slot).wait_send()

    for i in range(R):
        @pl.loop(0, T)
        def _(t2):
            @pl.when(jnp.logical_not((t * R + i == f) & (t2 == t)))
            def _():
                pltpu.make_async_remote_copy(
                    src_ref=fin.at[0], dst_ref=out_at(i, t2), send_sem=fs.at[0],
                    recv_sem=fr.at[i, t2], device_id=(t * R + i, t2),
                    device_id_type=MESH).wait_recv()


def hidden_gradient(F, T, grad_out, down_q, scales):
    R, Z, U = F // T, F // X, T // CORES
    tb, kd = grad_out.shape
    hb = down_q.shape[0]
    hh, pb = hb // CORES, tb // U
    aligned = hh % 128 == 0
    out_shape = (tb, R * hb) if aligned else (R * CORES, tb, hh)
    wide_scales = jnp.repeat(scales.astype(jnp.float32), BLOCK, axis=1)
    any_spec = pl.BlockSpec(memory_space=pl.ANY)
    dma = pltpu.SemaphoreType.DMA
    out = pl.pallas_call(
        functools.partial(kernel, F, T, aligned),
        out_shape=jax.ShapeDtypeStruct(out_shape, jnp.bfloat16),
        in_specs=[any_spec, any_spec, pl.BlockSpec(memory_space=pltpu.VMEM)],
        out_specs=any_spec,
        scratch_shapes=[
            pltpu.VMEM((F, tb, CORES * kd), jnp.bfloat16),
            pltpu.VMEM((hb, kd), jnp.bfloat16),
            pltpu.VMEM((hh, CORES * kd), jnp.bfloat16),
            pltpu.VMEM((F, tb, hh), jnp.bfloat16),
            pltpu.VMEM((tb, hh), jnp.float32),
            pltpu.VMEM((F, pb, hh), jnp.float32),
            pltpu.VMEM((F, U, pb, hh), jnp.bfloat16),
            pltpu.VMEM((F, pb, hh), jnp.bfloat16),
            dma((3,)),
            dma((2,)),
            dma((F, CHUNKS)),
            dma((Z, CHUNKS)),
            dma((Z, CHUNKS)),
            dma((Z, CHUNKS)),
            dma((F, CHUNKS)),
            dma((F, CHUNKS)),
            dma((F, U)),
            dma((F, U)),
            dma((F,)),
            dma((R, T)),
        ],
        compiler_params=pltpu.CompilerParams(
            collective_id=0, has_side_effects=True, vmem_limit_bytes=58 * 2**20),
        cost_estimate=pl.CostEstimate(
            flops=2 * F * tb * kd * hb, bytes_accessed=2 * hb * (kd + R * tb),
            transcendentals=0),
    )(grad_out, down_q, wide_scales)
    if aligned:
        return out
    return out.transpose(1, 0, 2).reshape(tb, R * hb)


def on_device(F, T, grad_out, down_q, scales, gate_act, up_act):
    grad_hidden = hidden_gradient(F, T, grad_out, down_q, scales).astype(jnp.float32)
    gate_val = gate_act.astype(jnp.float32)
    sigmoid_gate = jax.nn.sigmoid(gate_val)
    grad_up = (grad_hidden * gate_val * sigmoid_gate).astype(jnp.bfloat16)
    slope = sigmoid_gate * (1.0 + gate_val * (1.0 - sigmoid_gate))
    grad_gate = (grad_hidden * up_act.astype(jnp.float32) * slope).astype(jnp.bfloat16)
    return (grad_gate, grad_up)


def solution(mesh):
    F, T = mesh.shape["fsdp"], mesh.shape["tp"]
    spec = P("fsdp", "tp")
    return jax.shard_map(
        functools.partial(on_device, F, T),
        mesh=mesh, in_specs=(spec,) * 5, out_specs=(spec, spec), check_vma=False)
```

```python
import functools
import math

import jax
import jax.numpy as jnp
from jax import lax
from jax.experimental import pallas as pl
from jax.experimental.pallas import tpu as pltpu
from jax.sharding import PartitionSpec as P

BLOCK = 128
X = 2
CORES = 2
CHUNKS = 2
LAG_X = 3
LAG_SUM = 2
MESH = pl.DeviceIdType.MESH


def kernel(F, T, aligned, a_ref, q_ref, s_ref, out_ref, ga, q, w, part, tile, acc, rbuf, fin,
           lsem, wsem, gr, up, dn, xs, sr, ss, ts, tr, fs, fr):
    R, Z, U = F // T, F // X, T // CORES
    tb, kd = a_ref.shape
    hb = q_ref.shape[0]
    hh = hb // CORES
    cb = tb // CHUNKS
    pb = cb // U
    f, t = lax.axis_index("fsdp"), lax.axis_index("tp")
    z, x = lax.div(f, X), lax.rem(f, X)
    u, c = lax.div(t, CORES), lax.rem(t, CORES)
    xpeer, sibling = f + 1 - 2 * x, t + 1 - 2 * c
    owner_t, owner_i = lax.div(f, R), lax.rem(f, R)
    to_self = owner_t == t
    mine = pl.ds(pl.multiple_of(c * kd, 128), kd)
    theirs = pl.ds(pl.multiple_of((1 - c) * kd, 128), kd)

    copy_a = pltpu.make_async_copy(a_ref, ga.at[f, :, mine], lsem.at[0])
    copy_q = pltpu.make_async_copy(q_ref, q, lsem.at[1])
    copy_a.start()
    copy_q.start()

    barrier = pltpu.get_barrier_semaphore()

    def greet(df, dt):
        pl.semaphore_signal(barrier, inc=1, device_id=(df, dt), device_id_type=MESH)

    @pl.when(z > 0)
    def _():
        greet(f - X, t)

    @pl.when(z < Z - 1)
    def _():
        greet(f + X, t)

    greet(xpeer, t)
    greet(f, sibling)

    def peer(o):
        return lax.rem(u + o, U)

    for o in range(1, U):
        greet(f, peer(o) * CORES + c)

    for i in range(R):
        @pl.loop(0, T)
        def _(t2):
            @pl.when(jnp.logical_not((t * R + i == f) & (t2 == t)))
            def _():
                greet(t * R + i, t2)

    waits = 2 + (U - 1) + F
    waits = waits + (z > 0).astype(jnp.int32) + (z < Z - 1).astype(jnp.int32)
    pl.semaphore_wait(barrier, waits - to_self.astype(jnp.int32))

    def shard(slot, j, lanes):
        return ga.at[slot, pl.ds(pl.multiple_of(j * cb, cb), cb), lanes]

    def gather_copy(zz, j, sem, df):
        slot = zz * X + x
        ref = shard(slot, j, mine)
        return pltpu.make_async_remote_copy(
            src_ref=ref, dst_ref=ref, send_sem=sem.at[zz, j],
            recv_sem=gr.at[slot, j], device_id=(df, t), device_id_type=MESH)

    def gather_recv(slot, j):
        ref = shard(slot, j, mine)
        pltpu.make_async_remote_copy(
            src_ref=ref, dst_ref=ref, send_sem=xs.at[0, 0],
            recv_sem=gr.at[slot, j], device_id=(xpeer, t), device_id_type=MESH).wait_recv()

    def share_copy(slot, j):
        ref = shard(slot, j, mine)
        return pltpu.make_async_remote_copy(
            src_ref=ref, dst_ref=ref, send_sem=ss.at[slot, j],
            recv_sem=sr.at[slot, j], device_id=(f, sibling), device_id_type=MESH)

    def share_recv(slot, j):
        ref = shard(slot, j, theirs)
        pltpu.make_async_remote_copy(
            src_ref=ref, dst_ref=ref, send_sem=ss.at[slot, j],
            recv_sem=sr.at[slot, j], device_id=(f, sibling), device_id_type=MESH).wait_recv()

    def forward(zz, j, act):
        @pl.when((zz <= z) & (z < Z - 1))
        def _():
            act(gather_copy(zz, j, up, f + X))

        @pl.when((zz >= z) & (z > 0))
        def _():
            act(gather_copy(zz, j, dn, f - X))

        act(gather_copy(zz, j, xs, xpeer))

    def piece(j, u2):
        return pl.ds(pl.multiple_of(j * cb + u2 * pb, pb), pb)

    def sum_copy(slot, j, u2):
        return pltpu.make_async_remote_copy(
            src_ref=part.at[slot, piece(j, u2), :], dst_ref=rbuf.at[slot, j, u],
            send_sem=ts.at[slot, j, u2], recv_sem=tr.at[slot, j, u],
            device_id=(f, u2 * CORES + c), device_id_type=MESH)

    def sum_recv(slot, j, u2):
        ref = rbuf.at[slot, j, u2]
        pltpu.make_async_remote_copy(
            src_ref=ref, dst_ref=ref, send_sem=ts.at[slot, j, u2],
            recv_sem=tr.at[slot, j, u2], device_id=(f, u2 * CORES + c),
            device_id_type=MESH).wait_recv()

    def out_at(i, j, t2):
        rows = piece(j, lax.div(t2, CORES))
        half = lax.rem(t2, CORES)
        if aligned:
            return out_ref.at[rows, pl.ds(pl.multiple_of(i * hb + half * hh, 128), hh)]
        return out_ref.at[i * CORES + half, rows, :]

    def fin_remote(slot, j):
        return pltpu.make_async_remote_copy(
            src_ref=fin.at[slot, j], dst_ref=out_at(owner_i, j, t), send_sem=fs.at[slot, j],
            recv_sem=fr.at[owner_i, j, t], device_id=(slot, owner_t), device_id_type=MESH)

    def fin_local(j):
        return pltpu.make_async_copy(fin.at[f, j], out_at(owner_i, j, t), lsem.at[2 + j])

    def multiply(slot, j):
        share_recv(slot, j)
        rows = pl.ds(j * cb, cb)
        for lo in range(0, hh, 256):
            n = min(256, hh - lo)
            prod = lax.dot_general(ga[slot, rows, :], w[lo:lo + n, :], (((1,), (1,)), ((), ())),
                                   preferred_element_type=jnp.float32)
            tile[:, lo:lo + n] = prod
            part[slot, rows, lo:lo + n] = prod.astype(jnp.bfloat16)
        for o in range(1, U):
            sum_copy(slot, j, peer(o)).start()
        acc[slot, j] = tile[pl.ds(pl.multiple_of(u * pb, pb), pb), :]

    def add_up(slot, j):
        for o in range(1, U):
            sum_recv(slot, j, peer(o))
        total = acc[slot, j]
        for o in range(1, U):
            total = total + rbuf[slot, j, peer(o)].astype(jnp.float32)
        fin[slot, j] = total.astype(jnp.bfloat16)

    def send_sum(slot, j):
        own = to_self & (slot == f)

        @pl.when(own)
        def _():
            fin_local(j).start()

        @pl.when(jnp.logical_not(own))
        def _():
            fin_remote(slot, j).start()

    def start(copy):
        copy.start()

    copy_a.wait()
    for j in range(CHUNKS):
        forward(z, j, start)
    for j in range(CHUNKS):
        share_copy(f, j).start()
    copy_q.wait()

    rows = math.gcd(hh, BLOCK)
    other = (1 - c) * hh
    give = pltpu.make_async_remote_copy(
        src_ref=q.at[pl.ds(pl.multiple_of(other, rows), hh), :], dst_ref=w.at[:, mine],
        send_sem=wsem.at[0], recv_sem=wsem.at[1], device_id=(f, sibling), device_id_type=MESH)

    def scaled(r):
        at = pl.ds(pl.multiple_of(r, rows), rows)
        return (q[at, :].astype(jnp.float32)
                * s_ref[pl.ds(lax.div(r, BLOCK), 1), :]).astype(jnp.bfloat16)

    @pl.loop(0, hh // rows)
    def _(b):
        r = other + b * rows
        q[pl.ds(pl.multiple_of(r, rows), rows), :] = scaled(r)

    give.start()

    @pl.loop(0, hh // rows)
    def _(b):
        w[pl.ds(pl.multiple_of(b * rows, rows), rows), mine] = scaled(c * hh + b * rows)

    pltpu.make_async_remote_copy(
        src_ref=q.at[pl.ds(pl.multiple_of(other, rows), hh), :], dst_ref=w.at[:, theirs],
        send_sem=wsem.at[0], recv_sem=wsem.at[1], device_id=(f, sibling),
        device_id_type=MESH).wait_recv()

    steps = 2 * Z - 1

    below, above = z, Z - 1 - z
    last = jnp.where(above >= below, 2 * above, 2 * below - 1)
    near = (below == above) | (below == above + 1)
    before_last = last - jnp.where(near, 1, 2)

    def when_valid(k, body):
        d = lax.div(k + 1, 2)
        zz = z + d * (1 - 2 * lax.rem(k, 2))

        @pl.when((k >= 0) & (k < steps) & (zz >= 0) & (zz < Z))
        def _():
            body(zz, k)

    def send_held(column):
        def body(zz, _):
            for j in range(CHUNKS):
                send_sum(zz * X + column, j)

        @pl.loop(0, steps)
        def _(k):
            @pl.when(k + LAG_SUM < last)
            def _():
                when_valid(k, body)

    def own_column(zz, k):
        slot = zz * X + x
        for j in range(CHUNKS):
            @pl.when(zz != z)
            def _():
                gather_recv(slot, j)
                forward(zz, j, start)
                share_copy(slot, j).start()

            multiply(slot, j)

    def other_column(zz, k):
        slot = zz * X + 1 - x
        for j in range(CHUNKS):
            gather_recv(slot, j)
            share_copy(slot, j).start()
            if j == 0:
                @pl.when(k == before_last)
                def _():
                    send_held(x)
            else:
                add_up(slot, j - 1)

                @pl.when(k == last)
                def _():
                    if j == 1:
                        send_held(1 - x)
                    send_sum(slot, j - 1)

            multiply(slot, j)

    def sum_own(zz, k):
        slot = zz * X + x
        for j in range(CHUNKS):
            add_up(slot, j)

            @pl.when(k + LAG_SUM >= last)
            def _():
                send_sum(slot, j)

    def sum_other(zz, k):
        slot = zz * X + 1 - x
        add_up(slot, CHUNKS - 1)

        @pl.when((k + LAG_SUM >= last) & (k < last))
        def _():
            for j in range(CHUNKS - 1):
                send_sum(slot, j)

        @pl.when(k + LAG_SUM >= last)
        def _():
            send_sum(slot, CHUNKS - 1)

    @pl.loop(0, steps + LAG_X + LAG_SUM)
    def _(i):
        when_valid(i, own_column)
        when_valid(i - LAG_X, other_column)
        when_valid(i - LAG_SUM, sum_own)
        when_valid(i - LAG_X - LAG_SUM, sum_other)

    give.wait_send()

    @pl.loop(0, Z)
    def _(zz):
        for j in range(CHUNKS):
            forward(zz, j, lambda copy: copy.wait_send())

    @pl.loop(0, F)
    def _(slot):
        for j in range(CHUNKS):
            share_copy(slot, j).wait_send()
        own = to_self & (slot == f)
        for j in range(CHUNKS):
            for o in range(1, U):
                sum_copy(slot, j, peer(o)).wait_send()

            @pl.when(own)
            def _():
                fin_local(j).wait()

            @pl.when(jnp.logical_not(own))
            def _():
                fin_remote(slot, j).wait_send()

    for i in range(R):
        @pl.loop(0, T)
        def _(t2):
            @pl.when(jnp.logical_not((t * R + i == f) & (t2 == t)))
            def _():
                for j in range(CHUNKS):
                    pltpu.make_async_remote_copy(
                        src_ref=fin.at[0, 0], dst_ref=out_at(i, j, t2), send_sem=fs.at[0, 0],
                        recv_sem=fr.at[i, j, t2], device_id=(t * R + i, t2),
                        device_id_type=MESH).wait_recv()


def hidden_gradient(F, T, grad_out, down_q, scales):
    R, Z, U = F // T, F // X, T // CORES
    tb, kd = grad_out.shape
    hb = down_q.shape[0]
    hh, cb = hb // CORES, tb // CHUNKS
    pb = cb // U
    aligned = hh % 128 == 0
    out_shape = (tb, R * hb) if aligned else (R * CORES, tb, hh)
    wide_scales = jnp.repeat(scales.astype(jnp.float32), BLOCK, axis=1)
    any_spec = pl.BlockSpec(memory_space=pl.ANY)
    dma = pltpu.SemaphoreType.DMA
    out = pl.pallas_call(
        functools.partial(kernel, F, T, aligned),
        out_shape=jax.ShapeDtypeStruct(out_shape, jnp.bfloat16),
        in_specs=[any_spec, any_spec, pl.BlockSpec(memory_space=pltpu.VMEM)],
        out_specs=any_spec,
        scratch_shapes=[
            pltpu.VMEM((F, tb, CORES * kd), jnp.bfloat16),
            pltpu.VMEM((hb, kd), jnp.bfloat16),
            pltpu.VMEM((hh, CORES * kd), jnp.bfloat16),
            pltpu.VMEM((F, tb, hh), jnp.bfloat16),
            pltpu.VMEM((cb, hh), jnp.float32),
            pltpu.VMEM((F, CHUNKS, pb, hh), jnp.float32),
            pltpu.VMEM((F, CHUNKS, U, pb, hh), jnp.bfloat16),
            pltpu.VMEM((F, CHUNKS, pb, hh), jnp.bfloat16),
            dma((2 + CHUNKS,)),
            dma((2,)),
            dma((F, CHUNKS)),
            dma((Z, CHUNKS)),
            dma((Z, CHUNKS)),
            dma((Z, CHUNKS)),
            dma((F, CHUNKS)),
            dma((F, CHUNKS)),
            dma((F, CHUNKS, U)),
            dma((F, CHUNKS, U)),
            dma((F, CHUNKS)),
            dma((R, CHUNKS, T)),
        ],
        compiler_params=pltpu.CompilerParams(
            collective_id=0, has_side_effects=True, vmem_limit_bytes=58 * 2**20),
        cost_estimate=pl.CostEstimate(
            flops=2 * F * tb * kd * hb, bytes_accessed=2 * hb * (kd + R * tb),
            transcendentals=0),
    )(grad_out, down_q, wide_scales)
    if aligned:
        return out
    return out.transpose(1, 0, 2).reshape(tb, R * hb)


def on_device(F, T, grad_out, down_q, scales, gate_act, up_act):
    grad_hidden = hidden_gradient(F, T, grad_out, down_q, scales).astype(jnp.float32)
    gate_val = gate_act.astype(jnp.float32)
    sigmoid_gate = jax.nn.sigmoid(gate_val)
    grad_up = (grad_hidden * gate_val * sigmoid_gate).astype(jnp.bfloat16)
    slope = sigmoid_gate * (1.0 + gate_val * (1.0 - sigmoid_gate))
    grad_gate = (grad_hidden * up_act.astype(jnp.float32) * slope).astype(jnp.bfloat16)
    return (grad_gate, grad_up)


def solution(mesh):
    F, T = mesh.shape["fsdp"], mesh.shape["tp"]
    spec = P("fsdp", "tp")
    return jax.shard_map(
        functools.partial(on_device, F, T),
        mesh=mesh, in_specs=(spec,) * 5, out_specs=(spec, spec), check_vma=False)
```

```python
import functools
import math

import jax
import jax.numpy as jnp
from jax import lax
from jax.experimental import pallas as pl
from jax.experimental.pallas import tpu as pltpu
from jax.sharding import PartitionSpec as P

BLOCK = 128
X = 2
CORES = 2
CHUNKS = 2
LAG_X = 3
LAG_SUM = 2
MESH = pl.DeviceIdType.MESH


def kernel(F, T, aligned, a_ref, q_ref, s_ref, out_ref, ga, q, w, part, tile, acc, rbuf, fin,
           lsem, wsem, gr, up, dn, xs, sr, ss, ts, tr, fs, fr):
    R, Z, U = F // T, F // X, T // CORES
    tb, kd = a_ref.shape
    hb = q_ref.shape[0]
    hh = hb // CORES
    cb = tb // CHUNKS
    pb = cb // U
    f, t = lax.axis_index("fsdp"), lax.axis_index("tp")
    z, x = lax.div(f, X), lax.rem(f, X)
    u, c = lax.div(t, CORES), lax.rem(t, CORES)
    xpeer, sibling = f + 1 - 2 * x, t + 1 - 2 * c
    owner_t, owner_i = lax.div(f, R), lax.rem(f, R)
    to_self = owner_t == t
    mine = pl.ds(pl.multiple_of(c * kd, 128), kd)
    theirs = pl.ds(pl.multiple_of((1 - c) * kd, 128), kd)

    copy_a = pltpu.make_async_copy(a_ref, ga.at[f, :, mine], lsem.at[0])
    copy_q = pltpu.make_async_copy(q_ref, q, lsem.at[1])
    copy_a.start()
    copy_q.start()

    barrier = pltpu.get_barrier_semaphore()

    def greet(df, dt):
        pl.semaphore_signal(barrier, inc=1, device_id=(df, dt), device_id_type=MESH)

    @pl.when(z > 0)
    def _():
        greet(f - X, t)

    @pl.when(z < Z - 1)
    def _():
        greet(f + X, t)

    greet(xpeer, t)
    greet(f, sibling)

    def peer(o):
        return lax.rem(u + o, U)

    for o in range(1, U):
        greet(f, peer(o) * CORES + c)

    for i in range(R):
        @pl.loop(0, T)
        def _(t2):
            @pl.when(jnp.logical_not((t * R + i == f) & (t2 == t)))
            def _():
                greet(t * R + i, t2)

    waits = 2 + (U - 1) + F
    waits = waits + (z > 0).astype(jnp.int32) + (z < Z - 1).astype(jnp.int32)
    pl.semaphore_wait(barrier, waits - to_self.astype(jnp.int32))

    def shard(slot, j, lanes):
        return ga.at[slot, pl.ds(pl.multiple_of(j * cb, cb), cb), lanes]

    def gather_copy(zz, j, sem, df):
        slot = zz * X + x
        ref = shard(slot, j, mine)
        return pltpu.make_async_remote_copy(
            src_ref=ref, dst_ref=ref, send_sem=sem.at[zz, j],
            recv_sem=gr.at[slot, j], device_id=(df, t), device_id_type=MESH)

    def gather_recv(slot, j):
        ref = shard(slot, j, mine)
        pltpu.make_async_remote_copy(
            src_ref=ref, dst_ref=ref, send_sem=xs.at[0, 0],
            recv_sem=gr.at[slot, j], device_id=(xpeer, t), device_id_type=MESH).wait_recv()

    def share_copy(slot, j):
        ref = shard(slot, j, mine)
        return pltpu.make_async_remote_copy(
            src_ref=ref, dst_ref=ref, send_sem=ss.at[slot, j],
            recv_sem=sr.at[slot, j], device_id=(f, sibling), device_id_type=MESH)

    def share_recv(slot, j):
        ref = shard(slot, j, theirs)
        pltpu.make_async_remote_copy(
            src_ref=ref, dst_ref=ref, send_sem=ss.at[slot, j],
            recv_sem=sr.at[slot, j], device_id=(f, sibling), device_id_type=MESH).wait_recv()

    def forward(zz, j, act):
        @pl.when((zz <= z) & (z < Z - 1))
        def _():
            act(gather_copy(zz, j, up, f + X))

        @pl.when((zz >= z) & (z > 0))
        def _():
            act(gather_copy(zz, j, dn, f - X))

        act(gather_copy(zz, j, xs, xpeer))

    def piece(j, u2):
        return pl.ds(pl.multiple_of(j * cb + u2 * pb, pb), pb)

    def sum_copy(slot, j, u2):
        return pltpu.make_async_remote_copy(
            src_ref=part.at[slot, piece(j, u2), :], dst_ref=rbuf.at[slot, j, u],
            send_sem=ts.at[slot, j, u2], recv_sem=tr.at[slot, j, u],
            device_id=(f, u2 * CORES + c), device_id_type=MESH)

    def sum_recv(slot, j, u2):
        ref = rbuf.at[slot, j, u2]
        pltpu.make_async_remote_copy(
            src_ref=ref, dst_ref=ref, send_sem=ts.at[slot, j, u2],
            recv_sem=tr.at[slot, j, u2], device_id=(f, u2 * CORES + c),
            device_id_type=MESH).wait_recv()

    def out_at(i, j, t2):
        rows = piece(j, lax.div(t2, CORES))
        half = lax.rem(t2, CORES)
        if aligned:
            return out_ref.at[rows, pl.ds(pl.multiple_of(i * hb + half * hh, 128), hh)]
        return out_ref.at[i * CORES + half, rows, :]

    def fin_remote(slot, j):
        return pltpu.make_async_remote_copy(
            src_ref=fin.at[slot, j], dst_ref=out_at(owner_i, j, t), send_sem=fs.at[slot, j],
            recv_sem=fr.at[owner_i, j, t], device_id=(slot, owner_t), device_id_type=MESH)

    def fin_local(j):
        return pltpu.make_async_copy(fin.at[f, j], out_at(owner_i, j, t), lsem.at[2 + j])

    def multiply(slot, first, count):
        for j in range(first, first + count):
            share_recv(slot, j)
        rows = pl.ds(first * cb, count * cb)
        for lo in range(0, hh, 256):
            n = min(256, hh - lo)
            prod = lax.dot_general(ga[slot, rows, :], w[lo:lo + n, :], (((1,), (1,)), ((), ())),
                                   preferred_element_type=jnp.float32)
            tile[rows, lo:lo + n] = prod
            part[slot, rows, lo:lo + n] = prod.astype(jnp.bfloat16)
        for j in range(first, first + count):
            for o in range(1, U):
                sum_copy(slot, j, peer(o)).start()
        for j in range(first, first + count):
            acc[slot, j] = tile[piece(j, u), :]

    def add_up(slot, j):
        for o in range(1, U):
            sum_recv(slot, j, peer(o))
        total = acc[slot, j]
        for o in range(1, U):
            total = total + rbuf[slot, j, peer(o)].astype(jnp.float32)
        fin[slot, j] = total.astype(jnp.bfloat16)

    def send_sum(slot, j):
        own = to_self & (slot == f)

        @pl.when(own)
        def _():
            fin_local(j).start()

        @pl.when(jnp.logical_not(own))
        def _():
            fin_remote(slot, j).start()

    def start(copy):
        copy.start()

    copy_a.wait()
    for j in range(CHUNKS):
        forward(z, j, start)
    for j in range(CHUNKS):
        share_copy(f, j).start()
    copy_q.wait()

    rows = math.gcd(hh, BLOCK)
    other = (1 - c) * hh
    give = pltpu.make_async_remote_copy(
        src_ref=q.at[pl.ds(pl.multiple_of(other, rows), hh), :], dst_ref=w.at[:, mine],
        send_sem=wsem.at[0], recv_sem=wsem.at[1], device_id=(f, sibling), device_id_type=MESH)

    def scaled(r):
        at = pl.ds(pl.multiple_of(r, rows), rows)
        return (q[at, :].astype(jnp.float32)
                * s_ref[pl.ds(lax.div(r, BLOCK), 1), :]).astype(jnp.bfloat16)

    @pl.loop(0, hh // rows)
    def _(b):
        r = other + b * rows
        q[pl.ds(pl.multiple_of(r, rows), rows), :] = scaled(r)

    give.start()

    @pl.loop(0, hh // rows)
    def _(b):
        w[pl.ds(pl.multiple_of(b * rows, rows), rows), mine] = scaled(c * hh + b * rows)

    pltpu.make_async_remote_copy(
        src_ref=q.at[pl.ds(pl.multiple_of(other, rows), hh), :], dst_ref=w.at[:, theirs],
        send_sem=wsem.at[0], recv_sem=wsem.at[1], device_id=(f, sibling),
        device_id_type=MESH).wait_recv()

    steps = 2 * Z - 1

    below, above = z, Z - 1 - z
    last = jnp.where(above >= below, 2 * above, 2 * below - 1)
    near = (below == above) | (below == above + 1)
    before_last = last - jnp.where(near, 1, 2)

    def when_valid(k, body):
        d = lax.div(k + 1, 2)
        zz = z + d * (1 - 2 * lax.rem(k, 2))

        @pl.when((k >= 0) & (k < steps) & (zz >= 0) & (zz < Z))
        def _():
            body(zz, k)

    def send_held(column):
        def body(zz, _):
            for j in range(CHUNKS):
                send_sum(zz * X + column, j)

        @pl.loop(0, steps)
        def _(k):
            @pl.when(k + LAG_SUM < last)
            def _():
                when_valid(k, body)

    def own_column(zz, k):
        slot = zz * X + x

        @pl.when(zz != z)
        def _():
            for j in range(CHUNKS):
                gather_recv(slot, j)
                forward(zz, j, start)
                share_copy(slot, j).start()

        multiply(slot, 0, CHUNKS)

    def other_column(zz, k):
        slot = zz * X + 1 - x

        @pl.when(k < last)
        def _():
            for j in range(CHUNKS):
                gather_recv(slot, j)
                share_copy(slot, j).start()

            @pl.when(k == before_last)
            def _():
                send_held(x)

            multiply(slot, 0, CHUNKS)

        @pl.when(k == last)
        def _():
            for j in range(CHUNKS):
                gather_recv(slot, j)
                share_copy(slot, j).start()
                if j > 0:
                    add_up(slot, j - 1)
                if j == CHUNKS - 1:
                    send_held(1 - x)
                if j > 0:
                    send_sum(slot, j - 1)
                multiply(slot, j, 1)

    def sum_own(zz, k):
        slot = zz * X + x
        for j in range(CHUNKS):
            add_up(slot, j)

            @pl.when(k + LAG_SUM >= last)
            def _():
                send_sum(slot, j)

    def sum_other(zz, k):
        slot = zz * X + 1 - x
        for j in range(CHUNKS - 1):
            @pl.when(k < last)
            def _():
                add_up(slot, j)

                @pl.when(k + LAG_SUM >= last)
                def _():
                    send_sum(slot, j)

        add_up(slot, CHUNKS - 1)

        @pl.when(k + LAG_SUM >= last)
        def _():
            send_sum(slot, CHUNKS - 1)

    @pl.loop(0, steps + LAG_X + LAG_SUM)
    def _(i):
        when_valid(i, own_column)
        when_valid(i - LAG_X - 1, sum_other)
        when_valid(i - LAG_X, other_column)
        when_valid(i - LAG_SUM, sum_own)

    give.wait_send()

    @pl.loop(0, Z)
    def _(zz):
        for j in range(CHUNKS):
            forward(zz, j, lambda copy: copy.wait_send())

    @pl.loop(0, F)
    def _(slot):
        for j in range(CHUNKS):
            share_copy(slot, j).wait_send()
        own = to_self & (slot == f)
        for j in range(CHUNKS):
            for o in range(1, U):
                sum_copy(slot, j, peer(o)).wait_send()

            @pl.when(own)
            def _():
                fin_local(j).wait()

            @pl.when(jnp.logical_not(own))
            def _():
                fin_remote(slot, j).wait_send()

    for i in range(R):
        @pl.loop(0, T)
        def _(t2):
            @pl.when(jnp.logical_not((t * R + i == f) & (t2 == t)))
            def _():
                for j in range(CHUNKS):
                    pltpu.make_async_remote_copy(
                        src_ref=fin.at[0, 0], dst_ref=out_at(i, j, t2), send_sem=fs.at[0, 0],
                        recv_sem=fr.at[i, j, t2], device_id=(t * R + i, t2),
                        device_id_type=MESH).wait_recv()


def hidden_gradient(F, T, grad_out, down_q, scales):
    R, Z, U = F // T, F // X, T // CORES
    tb, kd = grad_out.shape
    hb = down_q.shape[0]
    hh, cb = hb // CORES, tb // CHUNKS
    pb = cb // U
    aligned = hh % 128 == 0
    out_shape = (tb, R * hb) if aligned else (R * CORES, tb, hh)
    wide_scales = jnp.repeat(scales.astype(jnp.float32), BLOCK, axis=1)
    any_spec = pl.BlockSpec(memory_space=pl.ANY)
    dma = pltpu.SemaphoreType.DMA
    out = pl.pallas_call(
        functools.partial(kernel, F, T, aligned),
        out_shape=jax.ShapeDtypeStruct(out_shape, jnp.bfloat16),
        in_specs=[any_spec, any_spec, pl.BlockSpec(memory_space=pltpu.VMEM)],
        out_specs=any_spec,
        scratch_shapes=[
            pltpu.VMEM((F, tb, CORES * kd), jnp.bfloat16),
            pltpu.VMEM((hb, kd), jnp.bfloat16),
            pltpu.VMEM((hh, CORES * kd), jnp.bfloat16),
            pltpu.VMEM((F, tb, hh), jnp.bfloat16),
            pltpu.VMEM((tb, hh), jnp.float32),
            pltpu.VMEM((F, CHUNKS, pb, hh), jnp.float32),
            pltpu.VMEM((F, CHUNKS, U, pb, hh), jnp.bfloat16),
            pltpu.VMEM((F, CHUNKS, pb, hh), jnp.bfloat16),
            dma((2 + CHUNKS,)),
            dma((2,)),
            dma((F, CHUNKS)),
            dma((Z, CHUNKS)),
            dma((Z, CHUNKS)),
            dma((Z, CHUNKS)),
            dma((F, CHUNKS)),
            dma((F, CHUNKS)),
            dma((F, CHUNKS, U)),
            dma((F, CHUNKS, U)),
            dma((F, CHUNKS)),
            dma((R, CHUNKS, T)),
        ],
        compiler_params=pltpu.CompilerParams(
            collective_id=0, has_side_effects=True, vmem_limit_bytes=58 * 2**20),
        cost_estimate=pl.CostEstimate(
            flops=2 * F * tb * kd * hb, bytes_accessed=2 * hb * (kd + R * tb),
            transcendentals=0),
    )(grad_out, down_q, wide_scales)
    if aligned:
        return out
    return out.transpose(1, 0, 2).reshape(tb, R * hb)


def on_device(F, T, grad_out, down_q, scales, gate_act, up_act):
    grad_hidden = hidden_gradient(F, T, grad_out, down_q, scales).astype(jnp.float32)
    gate_val = gate_act.astype(jnp.float32)
    sigmoid_gate = jax.nn.sigmoid(gate_val)
    grad_up = (grad_hidden * gate_val * sigmoid_gate).astype(jnp.bfloat16)
    slope = sigmoid_gate * (1.0 + gate_val * (1.0 - sigmoid_gate))
    grad_gate = (grad_hidden * up_act.astype(jnp.float32) * slope).astype(jnp.bfloat16)
    return (grad_gate, grad_up)


def solution(mesh):
    F, T = mesh.shape["fsdp"], mesh.shape["tp"]
    spec = P("fsdp", "tp")
    return jax.shard_map(
        functools.partial(on_device, F, T),
        mesh=mesh, in_specs=(spec,) * 5, out_specs=(spec, spec), check_vma=False)
```
